256 devices in a mesh: dp: 64 (over y, z, core), mp: 4 (over x).
Axes of the slice: x: 4, y: 4, z: 8, core: 2. Of those that a mesh axis runs over, the one named last changes fastest.
Arguments:
- pool: bfloat16 [4096, 36864], P('dp', 'mp'), may hold values from -6 to 6
- send_slots: int32 [64, 64], P('dp'), may hold values from 0 to 63, each once within a row
- page_source: int32 [64, 40], P('dp'), may hold values from 0 to 63, as said below
- prefix_pages: int32 [64], P('dp'), may hold values from 10 to 40, as said below
- queries: bfloat16 [4096, 73728], P('dp', 'mp'), may hold values from -50 to 50
- suffix_kv: bfloat16 [4096, 576], P('dp'), may hold values from -6 to 6
- hidden_in: bfloat16 [4096, 7168], P('dp', 'mp'), may hold values from -6 to 6
- expert_ids: int32 [4096, 8], P('dp'), may hold values from 0 to 255, as said below
- expert_slots: int32 [4096, 8], P('dp'), may hold values from -1 to 3, as said below
- gate_weights: float32 [4096, 8], P('dp'), may hold values from 0.05 to 0.4
- w_gate_up: bfloat16 [64, 7168, 1024], P('dp', 'mp'), may hold values from -0.0625 to 0.0625
- w_down: bfloat16 [64, 512, 7168], P('dp', None, 'mp'), may hold values from -0.1875 to 0.1875
Outputs:
- context: bfloat16 [4096, 65536], P('dp', 'mp')
- moe_out: bfloat16 [4096, 7168], P('dp', 'mp')
The draws below stay inside these ranges and needn't reach their ends.
Inputs may be any that keep to these rules, and one draw needn't show every extreme that they name: `send_slots`: each row orders all 64 slots of the group's store. `page_source`: entry s + c: the page is position c of what group s sends to the request's group; no entry repeats within a row. `prefix_pages`: some group's request has exactly 40 pages. `expert_ids`: each row names 8 different experts. `expert_slots`: a live slot belongs to an id below 32; one group's assignments to one expert take slots 0, 1, 2 and so on in token order, and -1 marks ids of 32 or more and assignments past 4; in every draw some expert receives 4 rows from every group.
All inputs are finite; a program needn't handle non-finite values.
Results may differ from the reference program's by a relative error of at most 0.027.
Values may be sent and summed in bfloat16 or wider, within the bound.
A program may use at most 128 MiB of HBM per device.

```python
from functools import partial
import jax
import jax.numpy as jnp
from jax import lax

D = 7168
KVL = 512
H = 128
EXPERTS = 256
TOP = 8
FF_WIN = 1024
PAGE = 64
SUF = 64
CAP = 4
PMAX = 40
FFH = 512
C = 576
CAPP = 1
POOL_DEV = 64
EXP_IN = 32
TOKENS = 4096
N_DP = 64


def distinct_order(key, lead_shape, span_count):
    drawn = jax.random.randint(key, lead_shape + (span_count,), 0, 1 << 20)
    return drawn * span_count + jnp.arange(span_count, dtype=jnp.int32)


def routing(key):
    pick_key, hot_key, row_key = jax.random.split(key, 3)
    scores = distinct_order(pick_key, (TOKENS,), EXPERTS)
    hot_expert = jax.random.randint(hot_key, (), 0, EXP_IN)
    chosen_scores = distinct_order(row_key, (N_DP,), SUF)
    threshold = lax.top_k(chosen_scores, CAP)[0][:, CAP - 1:CAP]
    chosen = (chosen_scores >= threshold).reshape(TOKENS)
    boost = jnp.where(chosen[:, None] & (jnp.arange(EXPERTS, dtype=jnp.int32)[None, :] == hot_expert), 1 << 29, 0)
    expert_list = lax.top_k(scores + boost, TOP)[1].astype(jnp.int32)
    flat_ids = expert_list.reshape(N_DP, SUF * TOP)
    onehot = (flat_ids[:, :, None] == jnp.arange(EXP_IN, dtype=jnp.int32)).astype(jnp.int32)
    before = jnp.cumsum(onehot, axis=1) - onehot
    rank_in = jnp.sum(before * onehot, axis=2)
    within_cap = (flat_ids < EXP_IN) & (rank_in < CAP)
    slot_list = jnp.where(within_cap, rank_in, -1).reshape(TOKENS, TOP).astype(jnp.int32)
    return (expert_list, slot_list)


def draw_expert_ids(key, part):
    return routing(key)[0]


def draw_expert_slots(key, part):
    return routing(key)[1]


def draw_prefix_pages(key, part):
    key = jax.random.fold_in(key, 3)
    length_key, long_key = jax.random.split(key)
    lengths = jax.random.randint(length_key, (N_DP,), PMAX // 4, PMAX + 1)
    longest = jax.random.randint(long_key, (), 0, N_DP)
    return jnp.where(jnp.arange(N_DP, dtype=jnp.int32) == longest, PMAX, lengths).astype(jnp.int32)


def draw_page_source(key, part):
    key = jax.random.fold_in(key, 5)
    source_order = jnp.argsort(distinct_order(key, (N_DP,), N_DP), axis=1).astype(jnp.int32)
    first_row = source_order[0]
    leading = first_row[0]
    final_group = N_DP - 1
    adjusted = jnp.where(first_row == final_group, leading, jnp.where(jnp.arange(N_DP, dtype=jnp.int32) == 0, final_group, first_row))
    source_order = source_order.at[0].set(adjusted)
    block_index = jnp.arange(PMAX, dtype=jnp.int32) // CAPP
    within = jnp.arange(PMAX, dtype=jnp.int32) % CAPP
    return (source_order[:, block_index] * CAPP + within[None, :]).astype(jnp.int32)


def draw_suffix_kv(key, part):
    key = jax.random.fold_in(key, 7)
    values = jnp.clip(jax.random.normal(key, (TOKENS, C), jnp.float32), -6.0, 6.0)
    return values.astype(jnp.bfloat16)


def draw_queries(key, part):
    key = jax.random.fold_in(key, 9)
    values = 1.2 * jnp.clip(jax.random.normal(key, (TOKENS, H, C), jnp.float32), -6.0, 6.0)
    return values.reshape(TOKENS, H * C).astype(jnp.bfloat16)


def levels(own_key, dims, pieces, low, top_value):
    def one(axis_at, parts):
        heights = jax.random.uniform(jax.random.fold_in(jax.random.fold_in(own_key, 6), axis_at), (parts,), jnp.float32, low / len(pieces), top_value / len(pieces))
        return jnp.repeat(jnp.exp(heights), dims[axis_at] // parts).reshape((-1,) + (1,) * (len(dims) - axis_at - 1))

    loudness = one(*pieces[0])
    for cut in pieces[1:]:
        loudness = loudness * one(*cut)
    return loudness


def noise(stream_key, shape, deviation, reach, cuts=(), kind=jnp.bfloat16):
    values = jax.random.normal(stream_key, shape, jnp.float32) * deviation
    if len(cuts) > 0:
        values = levels(stream_key, shape, cuts, -0.22, 0.18) * values
    return jnp.clip(values, min=-reach, max=reach).astype(kind)


def setup_inputs(seed: int = 0) -> dict:
    splits = jax.random.split(jax.random.key(seed), 13)
    return {
        "pool": noise(splits[0], (N_DP * POOL_DEV, PAGE * C), 1.0, 6.0, ((0, 64), (1, 4))),
        "send_slots": jax.vmap(lambda own: jax.random.permutation(own, POOL_DEV))(jax.random.split(splits[1], N_DP)).reshape((N_DP, POOL_DEV)).astype(jnp.int32),
        "page_source": draw_page_source(jax.random.fold_in(splits[12], 71), 0),
        "prefix_pages": draw_prefix_pages(jax.random.fold_in(splits[12], 71), 0),
        "queries": draw_queries(jax.random.fold_in(splits[12], 71), 0),
        "suffix_kv": draw_suffix_kv(jax.random.fold_in(splits[12], 71), 0),
        "hidden_in": noise(splits[6], (TOKENS, D), 1.0, 6.0, ((0, 64), (1, 4))),
        "expert_ids": draw_expert_ids(jax.random.fold_in(splits[12], 71), 0),
        "expert_slots": draw_expert_slots(jax.random.fold_in(splits[12], 71), 0),
        "gate_weights": jnp.clip(0.05 + 0.35 * jax.random.uniform(splits[9], (TOKENS, TOP), jnp.float32) ** levels(splits[9], (TOKENS, TOP), ((0, 64),), -0.2, 0.2), 0.05, 0.4),
        "w_gate_up": noise(splits[10], (N_DP, D, 2 * FFH), D ** -0.5, 0.0625, ((0, 64), (1, 4))),
        "w_down": noise(splits[11], (N_DP, FFH, D), FF_WIN ** -0.5, 0.1875, ((0, 64), (2, 4))),
    }


score_scale = 192 ** -0.5


def group_context(group_index, pool, send_slots, page_source, prefix_pages, queries, suffix_kv):
    pool_pages = pool.reshape(N_DP, POOL_DEV, PAGE * C)
    source = page_source[group_index]
    anchor = source // CAPP
    within = source % CAPP
    pool_slot = send_slots[anchor, group_index * CAPP + within]
    page_rows = pool_pages[anchor, pool_slot]
    prefix = page_rows.reshape(PMAX * PAGE, C)
    suffix = lax.dynamic_slice_in_dim(suffix_kv, group_index * SUF, SUF, 0)
    asked = lax.dynamic_slice_in_dim(queries, group_index * SUF, SUF, 0).reshape(SUF, H, C)
    key_rows = jnp.concatenate([prefix, suffix], axis=0).astype(jnp.float32)
    scores = jnp.einsum("qhc,kc->qhk", asked.astype(jnp.float32), key_rows) * score_scale
    position = jnp.arange(PMAX * PAGE + SUF, dtype=jnp.int32)[None, :]
    query_row = jnp.arange(SUF, dtype=jnp.int32)[:, None]
    visible = jnp.where(position < PMAX * PAGE, position < prefix_pages[group_index] * PAGE, position - PMAX * PAGE <= query_row)
    scores = jnp.where(visible[:, None, :], scores, -jnp.inf)
    peak = jnp.max(scores, axis=-1, keepdims=True)
    weights = jnp.exp(scores - peak)
    totals = jnp.sum(weights, axis=-1, keepdims=True)
    rounded = lax.optimization_barrier(weights.astype(jnp.bfloat16)).astype(jnp.float32)
    context = jnp.einsum("qhk,kc->qhc", rounded, key_rows[:, :KVL]) / totals
    return context.astype(jnp.bfloat16).reshape(SUF, H * KVL)


def expert_rows(expert, hidden_in, expert_ids, expert_slots, w_gate_up, w_down):
    group_of = (jnp.arange(TOKENS, dtype=jnp.int32) // SUF)[:, None]
    visible = (expert_ids == expert) & (expert_slots >= 0)
    target = jnp.where(visible, group_of * CAP + expert_slots, N_DP * CAP).reshape(-1)
    token_index = jnp.broadcast_to(jnp.arange(TOKENS, dtype=jnp.int32)[:, None], (TOKENS, TOP)).reshape(-1)
    owner_row = jnp.zeros((N_DP * CAP + 1,), jnp.int32).at[target].set(token_index)
    filled = jnp.zeros((N_DP * CAP + 1,), jnp.int32).at[target].set(1)
    buffer = jnp.where(filled[:N_DP * CAP, None] > 0, hidden_in[owner_row[:N_DP * CAP]], jnp.zeros((), jnp.bfloat16))
    summed = None
    for member in range(2):
        preacts = jnp.dot(buffer, w_gate_up[2 * expert + member], preferred_element_type=jnp.float32)
        hidden = (jax.nn.silu(preacts[:, :FFH]) * preacts[:, FFH:]).astype(jnp.bfloat16)
        product = jnp.dot(hidden, w_down[2 * expert + member], preferred_element_type=jnp.float32)
        summed = product if member == 0 else summed + product
    return summed.astype(jnp.bfloat16)


def reference(pool, send_slots, page_source, prefix_pages, queries, suffix_kv, hidden_in, expert_ids, expert_slots, gate_weights, w_gate_up, w_down):
    context = lax.map(partial(group_context, pool=pool, send_slots=send_slots, page_source=page_source, prefix_pages=prefix_pages, queries=queries, suffix_kv=suffix_kv), jnp.arange(N_DP, dtype=jnp.int32))
    context = context.reshape(TOKENS, H * KVL)
    outputs = lax.map(partial(expert_rows, hidden_in=hidden_in, expert_ids=expert_ids, expert_slots=expert_slots, w_gate_up=w_gate_up, w_down=w_down), jnp.arange(EXP_IN, dtype=jnp.int32))
    group_of = jnp.arange(TOKENS, dtype=jnp.int32) // SUF
    mixed = jnp.zeros((TOKENS, D), jnp.float32)
    for column in range(TOP):
        slot_used = expert_slots[:, column]
        visible = slot_used >= 0
        chosen = outputs[jnp.where(visible, expert_ids[:, column], 0), jnp.where(visible, group_of * CAP + slot_used, 0)]
        mixed = mixed + jnp.where(visible, gate_weights[:, column], jnp.zeros((), jnp.float32))[:, None] * chosen.astype(jnp.float32)
    return context, mixed.astype(jnp.bfloat16)
```

```python
import functools

import jax
import jax.numpy as jnp
from jax import lax
from jax.experimental import pallas as pl
from jax.experimental.pallas import tpu as pltpu
from jax.sharding import PartitionSpec as P

MESH = pl.DeviceIdType.MESH
BF = jnp.bfloat16
F32 = jnp.float32
I32 = jnp.int32

KVL = 512
ENT = 576
PAGE = 64
CAP = 4
CHIPS = 32
HALF = 896
CHUNKS = 5
KEYS = 256
WIDE = 1152
HEADS = 32
ROWS = 2048
BLK = 512
LOW = -1e30
GAIN = 192 ** (-0.5) * 1.4426950408889634
FIRST = 16
STEP = 4


def dot(a, b):
    return jnp.dot(a, b, preferred_element_type=F32)


def dot_nt(a, b):
    return lax.dot_general(a, b, (((1,), (1,)), ((), ())), preferred_element_type=F32)


def iota(shape, axis):
    return lax.broadcasted_iota(I32, shape, axis)


def kernel(
    pool_h, slots_s, source_v, pages_s, queries_h, suffix_v, hidden_v, ids_v, exp_slots_v, gates_v, wgu_h, wdn_h,
    context_h, moe_v,
    pool, tmp_lat, tmp_rope, send_p, arr, fwd, work, keys, q_a, q_b, suf_k, acc, peak, total, out, q_raw,
    wgu, wdn, disp, got, part, rsb, hid, pf, pxs, pxr, ret_s, ret_r, mixw, order_v, order_s,
    ld, disp_ss, disp_rs, page_ss, page_rs, fwd_ss, fwd_rs, sib_ss, sib_rs, x_ss, x_rs, ret_ss, ret_rs, ag_ss, ag_rs,
):
    dp = lax.axis_index("dp")
    mp = lax.axis_index("mp")
    core = lax.rem(dp, 2)
    chip = dp // 2
    y = chip // 8
    z = lax.rem(chip, 8)
    other = 1 - core
    sibling = (chip * 2 + other, mp)

    def shift(k):
        dz = lax.rem(3 * k, 8)
        dy = lax.rem(k // 8 + k, 4)
        return dy, dz

    def to_chip(k):
        dy, dz = shift(k)
        return lax.rem(y + dy, 4) * 8 + lax.rem(z + dz, 8)

    def from_chip(k):
        dy, dz = shift(k)
        return lax.rem(y + 4 - dy, 4) * 8 + lax.rem(z + 8 - dz, 8)

    def x_peer(step):
        return (dp, lax.rem(mp + step, 4))

    barrier = pltpu.get_barrier_semaphore()

    def greet(k, carry):
        pl.semaphore_signal(barrier, inc=1, device_id=(to_chip(k) * 2 + core, mp), device_id_type=MESH)
        return carry

    lax.fori_loop(1, CHIPS, greet, 0)
    pl.semaphore_signal(barrier, inc=1, device_id=sibling, device_id_type=MESH)
    for step in (1, 2, 3):
        pl.semaphore_signal(barrier, inc=1, device_id=x_peer(step), device_id_type=MESH)

    load_pool = pltpu.make_async_copy(pool_h, pool, ld.at[0])
    load_pool.start()
    load_q = pltpu.make_async_copy(queries_h, q_raw, ld.at[1])
    load_q.start()
    load_gu = pltpu.make_async_copy(wgu_h.at[0], wgu, ld.at[2])
    load_gu.start()
    load_dn = pltpu.make_async_copy(wdn_h.at[0], wdn, ld.at[3])
    load_dn.start()

    src = source_v[...]
    src_y = src // 16
    src_z = lax.rem(src // 2, 8)
    res = lax.rem(3 * lax.rem(z + 8 - src_z, 8), 8)
    lap = lax.rem(lax.rem(y + 4 - src_y, 4) + 8 - res, 4)
    lane40 = iota((1, 40), 1)
    rank_key = (lap * 8 + res) * 64 + lane40
    sub = iota((40, 40), 0)
    lane = iota((40, 40), 1)
    key_rows = jnp.broadcast_to(rank_key, (40, 40))
    key_cols = jnp.sum(jnp.where(sub == lane, key_rows, 0), axis=1, keepdims=True)
    rank_col = jnp.sum(jnp.where(key_rows < key_cols, 1, 0), axis=1, keepdims=True)
    src_col = jnp.sum(jnp.where(sub == lane, jnp.broadcast_to(src, (40, 40)), 0), axis=1, keepdims=True)
    hit = iota((40, 128), 1) == rank_col
    seen_col = jnp.where(iota((40, 128), 0) < pages_s[0], 1, 0)
    ordered = jnp.sum(jnp.where(hit, src_col, 0), axis=0, keepdims=True)
    seen = jnp.sum(jnp.where(hit, seen_col, 0), axis=0, keepdims=True)
    row8 = iota((8, 128), 0)
    order_v[...] = jnp.where(row8 == 0, ordered, jnp.where(row8 == 1, seen, 0))
    order_copy = pltpu.make_async_copy(order_v, order_s, ld.at[4])
    order_copy.start()

    ids = ids_v[...]
    exp_slots = exp_slots_v[...]
    target = jnp.where((exp_slots >= 0) & (ids < CHIPS), ids * CAP + exp_slots, -1)
    half_lane = iota((8, 128), 1) // 64
    target = jnp.concatenate([target, target], axis=1)
    target = jnp.where(target >= 0, target * 2 + half_lane, -1)
    gates = jnp.concatenate([gates_v[...], gates_v[...]], axis=1)
    row = iota((256, 128), 0)
    wanted = ((row // 8) * 4 + lax.rem(row, 4)) * 2 + lax.rem(row // 4, 2)
    select = jnp.zeros((256, 128), F32)
    mix = jnp.zeros((256, 128), F32)
    for k in range(8):
        match = wanted == target[k : k + 1, :]
        select = select + jnp.where(match, 1.0, 0.0)
        mix = mix + jnp.where(match, gates[k : k + 1, :], 0.0)
    mixw[...] = mix
    hidden = hidden_v[...]
    halves = jnp.concatenate([hidden[:, :HALF], hidden[:, HALF:]], axis=0)
    picked = dot(select.astype(BF), halves)
    disp[...] = picked.reshape(CHIPS, 8, HALF).astype(BF)

    pl.semaphore_wait(barrier, CHIPS + 3)

    def disp_copy(k, q):
        return pltpu.make_async_remote_copy(
            src_ref=disp.at[q], dst_ref=got.at[core, chip], send_sem=disp_ss.at[k], recv_sem=disp_rs.at[k],
            device_id=(q * 2 + core, mp), device_id_type=MESH,
        )

    def disp_start(k, carry):
        disp_copy(k, to_chip(k)).start()
        return carry

    lax.fori_loop(1, CHIPS, disp_start, 0)
    got[core, chip] = disp[chip]

    load_pool.wait()
    perm_row = iota((256, 256), 0)
    perm_col = iota((256, 256), 1)
    perm = jnp.where((lax.rem(perm_row, 16) == perm_col // 16) & (perm_row // 16 == lax.rem(perm_col, 16)), 1.0, 0.0).astype(BF)
    for g in range(4):
        lat_rows = []
        rope_rows = []
        for t in range(16):
            start = t * ENT
            lat_rows.append(pool[g * 16 : g * 16 + 16, start : start + KVL])
            rope = pool[g * 16 : g * 16 + 16, start + KVL : start + ENT]
            rope_rows.append(jnp.concatenate([rope, rope], axis=1))
        lat = dot(perm, jnp.concatenate(lat_rows, axis=0)).astype(BF)
        rope = dot(perm, jnp.concatenate(rope_rows, axis=0)).astype(BF)
        for p in range(16):
            for c in range(4):
                tmp_lat[g * 16 + p, c * 16 : c * 16 + 16, :] = lat[p * 16 : p * 16 + 16, c * 128 : c * 128 + 128]
            tmp_rope[g * 16 + p] = rope[p * 16 : p * 16 + 16, :]

    low_lane = iota((16, 128), 1) < 64

    def page_copy(k, q):
        return pltpu.make_async_remote_copy(
            src_ref=send_p.at[q], dst_ref=arr.at[chip], send_sem=page_ss.at[k], recv_sem=page_rs.at[k],
            device_id=(q * 2 + core, mp), device_id_type=MESH,
        )

    def page_fill(q):
        first = slots_s[0, 2 * q]
        second = slots_s[0, 2 * q + 1]
        send_p[q, 0:64, :] = tmp_lat[first]
        send_p[q, 64:80, :] = jnp.where(low_lane, tmp_rope[first], tmp_rope[second])
        send_p[q, 80:144, :] = tmp_lat[second]

    def page_start(k, carry):
        q = to_chip(k)
        page_fill(q)
        page_copy(k, q).start()
        return carry

    lax.fori_loop(1, CHIPS, page_start, 0)
    page_fill(chip)
    arr[chip] = send_p[chip]

    load_q.wait()
    zeros = jnp.zeros((64, 64), BF)
    for h in range(HEADS):
        rows = slice(h * 64, h * 64 + 64)
        start = h * ENT
        lat = q_raw[:, start : start + KVL]
        rope = q_raw[:, start + KVL : start + ENT]
        q_a[rows, 0:KVL] = lat
        q_a[rows, KVL : KVL + 128] = jnp.concatenate([rope, zeros], axis=1)
        q_b[rows, 0:128] = jnp.concatenate([zeros, rope], axis=1)
        q_b[rows, 128 : 128 + KVL] = lat

    suf_k[:, 0:KVL] = suffix_v[:, 0:KVL]
    suf_k[:, KVL : KVL + 128] = jnp.concatenate([suffix_v[:, KVL:ENT], zeros], axis=1)

    def suffix_block(b, carry):
        rows = pl.ds(pl.multiple_of(b * BLK, BLK), BLK)
        s = dot_nt(q_a[rows, :], suf_k[...]) * GAIN
        token = lax.rem(iota((BLK, 64), 0), 64)
        s = jnp.where(iota((BLK, 64), 1) <= token, s, LOW)
        top = jnp.max(s, axis=1, keepdims=True)
        w = jnp.exp2(s - top)
        peak[rows, :] = jnp.broadcast_to(top, (BLK, 128))
        total[rows, :] = jnp.concatenate([w, jnp.zeros((BLK, 64), F32)], axis=1)
        acc[rows, :] = dot(w.astype(BF), suf_k[:, 0:KVL])
        return carry

    lax.fori_loop(0, ROWS // BLK, suffix_block, 0)

    def forward_copy(k, q):
        return pltpu.make_async_remote_copy(
            src_ref=arr.at[q, pl.ds(pl.multiple_of(64 * other, 16), 80)], dst_ref=fwd.at[q],
            send_sem=fwd_ss.at[k], recv_sem=fwd_rs.at[k], device_id=sibling, device_id_type=MESH,
        )

    def arrive(k, carry):
        q = from_chip(k)
        page_copy(k, q).wait_recv()
        forward_copy(k, q).start()
        return carry

    def arrivals(stage):
        if stage == 0:
            forward_copy(0, chip).start()
            lax.fori_loop(1, FIRST, arrive, 0)
        else:
            lax.fori_loop(FIRST + STEP * (stage - 1), FIRST + STEP * stage, arrive, 0)

    def both_halves(tile):
        wide = tile.astype(F32)
        turned = pltpu.roll(wide, 64, 1)
        keep = (iota((16, 128), 1) // 64) == core
        return jnp.where(keep, wide, turned).astype(BF)

    def settle(k, carry):
        q = from_chip(k)
        forward_copy(k, q).wait_recv()
        work[0, q, 0:64, :] = arr[q, pl.ds(pl.multiple_of(80 * core, 16), 64), :]
        work[0, q, 64:80, :] = both_halves(arr[q, 64:80, :])
        work[1, q, 0:64, :] = fwd[q, pl.ds(pl.multiple_of(16 * core, 16), 64), :]
        work[1, q, 64:80, :] = both_halves(fwd[q, pl.ds(pl.multiple_of(64 * other, 16), 16), :])
        return carry

    mine = pl.ds(pl.multiple_of(mp * 64, 64), 64)

    def near_copy(ch, step):
        way = 0 if step == 1 else 1
        return pltpu.make_async_remote_copy(
            src_ref=keys.at[ch, mine], dst_ref=keys.at[ch, mine], send_sem=ag_ss.at[ch, way], recv_sem=ag_rs.at[ch, way],
            device_id=x_peer(step), device_id_type=MESH,
        )

    def far_copy(ch, step):
        way = 2 if step == 1 else 3
        owner = lax.rem(mp + 4 - step, 4)
        begin = owner * 64 + (0 if step == 1 else 32)
        rows = pl.ds(pl.multiple_of(begin, 32), 32)
        return pltpu.make_async_remote_copy(
            src_ref=keys.at[ch, rows], dst_ref=keys.at[ch, rows], send_sem=ag_ss.at[ch, way], recv_sem=ag_rs.at[ch, way],
            device_id=x_peer(step), device_id_type=MESH,
        )

    def gather_chunk(ch):
        if ch == 0:
            lax.fori_loop(0, FIRST, settle, 0)
        else:
            lax.fori_loop(FIRST + STEP * (ch - 1), FIRST + STEP * ch, settle, 0)

        def pick(i, carry):
            a = jnp.clip(order_s[0, ch * 8 + i], 0, 63)
            b = jnp.clip(order_s[0, ch * 8 + 4 + i], 0, 63)
            rel_a = lax.rem(lax.rem(a, 2) + core, 2)
            rel_b = lax.rem(lax.rem(b, 2) + core, 2)
            page_a = work[rel_a, a // 2]
            page_b = work[rel_b, b // 2]
            rows = pl.ds(pl.multiple_of(mp * 64 + i * 16, 16), 16)
            for c in range(4):
                keys[ch, rows, c * 128 : c * 128 + 128] = page_a[c * 16 : c * 16 + 16, :]
                keys[ch, rows, 640 + c * 128 : 640 + c * 128 + 128] = page_b[c * 16 : c * 16 + 16, :]
            keys[ch, rows, 512:640] = jnp.where(low_lane, page_a[64:80, :], page_b[64:80, :])
            return carry

        lax.fori_loop(0, 4, pick, 0)
        near_copy(ch, 1).start()
        near_copy(ch, 3).start()

    def relay_chunk(ch):
        near_copy(ch, 1).wait_recv()
        far_copy(ch, 1).start()
        near_copy(ch, 3).wait_recv()
        far_copy(ch, 3).start()

    def attend_chunk(ch):
        far_copy(ch, 1).wait_recv()
        far_copy(ch, 3).wait_recv()
        page_lane = lax.rem(iota((1, KEYS), 1) // 16, 4)

        def bias(base):
            value = jnp.zeros((1, KEYS), F32)
            for i in range(4):
                shown = order_s[1, ch * 8 + base + i].astype(F32)
                value = jnp.where(page_lane == i, (shown - 1.0) * -LOW, value)
            return value

        bias_a = bias(0)
        bias_b = bias(4)

        def block(b, carry):
            rows = pl.ds(pl.multiple_of(b * BLK, BLK), BLK)
            s_a = dot_nt(q_a[rows, :], keys[ch, :, 0:640]) * GAIN + bias_a
            s_b = dot_nt(q_b[rows, :], keys[ch, :, 512:1152]) * GAIN + bias_b
            old = peak[rows, 0:1]
            top = jnp.maximum(jnp.max(jnp.maximum(s_a, s_b), axis=1, keepdims=True), old)
            factor = jnp.exp2(old - top)
            w_a = jnp.exp2(s_a - top)
            w_b = jnp.exp2(s_b - top)
            both = w_a + w_b
            peak[rows, :] = jnp.broadcast_to(top, (BLK, 128))
            total[rows, :] = total[rows, :] * factor + both[:, 0:128] + both[:, 128:256]
            acc[rows, :] = (
                acc[rows, :] * factor
                + dot(w_a.astype(BF), keys[ch, :, 0:KVL])
                + dot(w_b.astype(BF), keys[ch, :, 640 : 640 + KVL])
            )
            return carry

        lax.fori_loop(0, ROWS // BLK, block, 0)

    def disp_wait(k, carry):
        disp_copy(k, to_chip(k)).wait_recv()
        return carry

    lax.fori_loop(1, CHIPS, disp_wait, 0)
    got_copy = pltpu.make_async_remote_copy(
        src_ref=got.at[core], dst_ref=got.at[core], send_sem=sib_ss.at[0], recv_sem=sib_rs.at[0],
        device_id=sibling, device_id_type=MESH,
    )
    got_copy.start()
    load_gu.wait()
    got_copy.wait_recv()
    rows512 = got[...].astype(F32).reshape(512, HALF).astype(BF)
    pr = iota((256, 512), 0)
    pc = iota((256, 512), 1)
    same = (pr // 4 == pc // 8) & (lax.rem(pr, 4) == lax.rem(pc, 4))
    left = dot(jnp.where(same & (lax.rem(pc // 4, 2) == 0), 1.0, 0.0).astype(BF), rows512).astype(BF)
    right = dot(jnp.where(same & (lax.rem(pc // 4, 2) == 1), 1.0, 0.0).astype(BF), rows512).astype(BF)
    part[...] = (dot(left, wgu[0:HALF, :]) + dot(right, wgu[HALF : 2 * HALF, :])).astype(BF)

    def sum_copy(step):
        there = lax.rem(mp + step, 4)
        return pltpu.make_async_remote_copy(
            src_ref=part.at[pl.ds(pl.multiple_of(there * 64, 64), 64)], dst_ref=rsb.at[mp],
            send_sem=x_ss.at[step - 1], recv_sem=x_rs.at[step - 1], device_id=x_peer(step), device_id_type=MESH,
        )

    for step in (2, 1, 3):
        sum_copy(step).start()
    rsb[mp] = part[mine, :]

    arrivals(0)

    for step in (1, 2, 3):
        sum_copy(step).wait_recv()
    pre = rsb[0].astype(F32) + rsb[1].astype(F32) + rsb[2].astype(F32) + rsb[3].astype(F32)
    gate = pre[:, 0:512]
    hid[mine, :] = (gate / (1.0 + jnp.exp(-gate)) * pre[:, 512:1024]).astype(BF)

    def hid_copy(step):
        return pltpu.make_async_remote_copy(
            src_ref=hid.at[mine], dst_ref=hid.at[mine],
            send_sem=x_ss.at[step + 2], recv_sem=x_rs.at[step + 2], device_id=x_peer(step), device_id_type=MESH,
        )

    for step in (2, 1, 3):
        hid_copy(step).start()

    order_copy.wait()
    gather_chunk(0)

    for step in (1, 2, 3):
        hid_copy(step).wait_recv()
    load_dn.wait()
    dr = iota((512, 256), 0)
    dc = iota((512, 256), 1)
    twice = jnp.where((dr // 8 == dc // 4) & (lax.rem(dr, 4) == lax.rem(dc, 4)), 1.0, 0.0).astype(BF)
    doubled = dot(twice, hid[...]).astype(BF)
    is_left = lax.rem(iota((512, HALF), 0) // 4, 2) == 0
    pf[...] = jnp.where(is_left, dot(doubled, wdn[:, 0:HALF]), dot(doubled, wdn[:, HALF : 2 * HALF])).reshape(2, 256, HALF)
    pxs[...] = pf[other].astype(BF)
    part_copy = pltpu.make_async_remote_copy(
        src_ref=pxs, dst_ref=pxr, send_sem=sib_ss.at[1], recv_sem=sib_rs.at[1], device_id=sibling, device_id_type=MESH,
    )
    part_copy.start()

    arrivals(1)
    part_copy.wait_recv()
    ret_s[...] = (pf[core] + pxr[...].astype(F32)).reshape(CHIPS, 8, HALF).astype(BF)

    def ret_copy(k, q):
        return pltpu.make_async_remote_copy(
            src_ref=ret_s.at[q], dst_ref=ret_r.at[chip], send_sem=ret_ss.at[k], recv_sem=ret_rs.at[k],
            device_id=(q * 2 + core, mp), device_id_type=MESH,
        )

    def ret_start(k, carry):
        ret_copy(k, to_chip(k)).start()
        return carry

    lax.fori_loop(1, CHIPS, ret_start, 0)
    ret_r[chip] = ret_s[chip]

    gather_chunk(1)
    relay_chunk(0)
    arrivals(2)
    gather_chunk(2)
    relay_chunk(1)
    arrivals(3)
    gather_chunk(3)
    attend_chunk(0)
    relay_chunk(2)
    arrivals(4)
    gather_chunk(4)
    attend_chunk(1)
    relay_chunk(3)
    attend_chunk(2)
    relay_chunk(4)
    attend_chunk(3)

    def ret_wait(k, carry):
        ret_copy(k, to_chip(k)).wait_recv()
        return carry

    lax.fori_loop(1, CHIPS, ret_wait, 0)
    rows256 = ret_r[...].astype(F32).reshape(256, HALF).astype(BF)
    weights = mixw[...]
    high = weights.astype(BF)
    low = (weights - high.astype(F32)).astype(BF)
    dims = (((0,), (0,)), ((), ()))
    mixed = lax.dot_general(high, rows256, dims, preferred_element_type=F32) + lax.dot_general(
        low, rows256, dims, preferred_element_type=F32
    )
    moe_v[:, 0:HALF] = mixed[0:64].astype(BF)
    moe_v[:, HALF : 2 * HALF] = mixed[64:128].astype(BF)

    attend_chunk(4)

    for h in range(HEADS):
        rows = slice(h * 64, h * 64 + 64)
        whole = jnp.sum(total[rows, :], axis=1, keepdims=True)
        out[:, h * KVL : h * KVL + KVL] = (acc[rows, :] / whole).astype(BF)
    store = pltpu.make_async_copy(out, context_h, ld.at[5])
    store.start()

    def sent(k, carry):
        disp_copy(k, to_chip(k)).wait_send()
        page_copy(k, to_chip(k)).wait_send()
        forward_copy(k, from_chip(k)).wait_send()
        ret_copy(k, to_chip(k)).wait_send()
        return carry

    lax.fori_loop(1, CHIPS, sent, 0)
    forward_copy(0, chip).wait_send()
    got_copy.wait_send()
    part_copy.wait_send()
    for step in (1, 2, 3):
        sum_copy(step).wait_send()
        hid_copy(step).wait_send()
    for ch in range(CHUNKS):
        for step in (1, 3):
            near_copy(ch, step).wait_send()
            far_copy(ch, step).wait_send()
    store.wait()


def body(
    pool, send_slots, page_source, prefix_pages, queries, suffix_kv, hidden_in,
    expert_ids, expert_slots, gate_weights, w_gate_up, w_down,
):
    any_spec = pl.BlockSpec(memory_space=pl.ANY)
    vmem = pl.BlockSpec(memory_space=pltpu.VMEM)
    smem = pl.BlockSpec(memory_space=pltpu.SMEM)
    dma = pltpu.SemaphoreType.DMA
    scratch = [
        pltpu.VMEM((64, 9216), BF),
        pltpu.VMEM((64, 64, 128), BF),
        pltpu.VMEM((64, 16, 128), BF),
        pltpu.VMEM((CHIPS, 144, 128), BF),
        pltpu.VMEM((CHIPS, 144, 128), BF),
        pltpu.VMEM((CHIPS, 80, 128), BF),
        pltpu.VMEM((2, CHIPS, 80, 128), BF),
        pltpu.VMEM((CHUNKS, KEYS, WIDE), BF),
        pltpu.VMEM((ROWS, 640), BF),
        pltpu.VMEM((ROWS, 640), BF),
        pltpu.VMEM((64, 640), BF),
        pltpu.VMEM((ROWS, KVL), F32),
        pltpu.VMEM((ROWS, 128), F32),
        pltpu.VMEM((ROWS, 128), F32),
        pltpu.VMEM((64, HEADS * KVL), BF),
        pltpu.VMEM((64, HEADS * ENT), BF),
        pltpu.VMEM((2 * HALF, 1024), BF),
        pltpu.VMEM((512, 2 * HALF), BF),
        pltpu.VMEM((CHIPS, 8, HALF), BF),
        pltpu.VMEM((2, CHIPS, 8, HALF), BF),
        pltpu.VMEM((256, 1024), BF),
        pltpu.VMEM((4, 64, 1024), BF),
        pltpu.VMEM((256, 512), BF),
        pltpu.VMEM((2, 256, HALF), F32),
        pltpu.VMEM((256, HALF), BF),
        pltpu.VMEM((256, HALF), BF),
        pltpu.VMEM((CHIPS, 8, HALF), BF),
        pltpu.VMEM((CHIPS, 8, HALF), BF),
        pltpu.VMEM((256, 128), F32),
        pltpu.VMEM((8, 128), I32),
        pltpu.SMEM((8, 128), I32),
        dma((6,)),
        dma((CHIPS,)), dma((CHIPS,)),
        dma((CHIPS,)), dma((CHIPS,)),
        dma((CHIPS,)), dma((CHIPS,)),
        dma((2,)), dma((2,)),
        dma((6,)), dma((6,)),
        dma((CHIPS,)), dma((CHIPS,)),
        dma((CHUNKS, 4)), dma((CHUNKS, 4)),
    ]
    context, moe_out = pl.pallas_call(
        kernel,
        out_shape=(
            jax.ShapeDtypeStruct((64, HEADS * KVL), BF),
            jax.ShapeDtypeStruct((64, 2 * HALF), BF),
        ),
        in_specs=[any_spec, smem, vmem, smem, any_spec, vmem, vmem, vmem, vmem, vmem, any_spec, any_spec],
        out_specs=(any_spec, vmem),
        scratch_shapes=scratch,
        compiler_params=pltpu.CompilerParams(
            collective_id=0, has_side_effects=True, vmem_limit_bytes=56 * 2**20
        ),
        name="prefill",
    )(
        pool, send_slots, page_source, prefix_pages, queries, suffix_kv, hidden_in,
        expert_ids.T, expert_slots.T, gate_weights.T, w_gate_up, w_down,
    )
    return context, moe_out


def solution(mesh):
    return jax.shard_map(
        body,
        mesh=mesh,
        in_specs=(
            P("dp", "mp"),
            P("dp", None),
            P("dp", None),
            P("dp"),
            P("dp", "mp"),
            P("dp", None),
            P("dp", "mp"),
            P("dp", None),
            P("dp", None),
            P("dp", None),
            P("dp", "mp", None),
            P("dp", None, "mp"),
        ),
        out_specs=(P("dp", "mp"), P("dp", "mp")),
        check_vma=False,
    )
```

```python
import functools

import jax
import jax.numpy as jnp
from jax import lax
from jax.experimental import pallas as pl
from jax.experimental.pallas import tpu as pltpu
from jax.sharding import PartitionSpec as P

MESH = pl.DeviceIdType.MESH
BF = jnp.bfloat16
F32 = jnp.float32
I32 = jnp.int32

KVL = 512
ENT = 576
PAGE = 64
CAP = 4
CHIPS = 32
HALF = 896
CHUNKS = 5
KEYS = 256
WIDE = 1152
HEADS = 32
ROWS = 2048
BLK = 512
LOW = -1e30
GAIN = 192 ** (-0.5) * 1.4426950408889634
FIRST = 16
STEP = 4
PRE = 1


def dot(a, b):
    return jnp.dot(a, b, preferred_element_type=F32)


def dot_nt(a, b):
    return lax.dot_general(a, b, (((1,), (1,)), ((), ())), preferred_element_type=F32)


def iota(shape, axis):
    return lax.broadcasted_iota(I32, shape, axis)


def kernel(
    pool_h, slots_s, source_v, pages_s, queries_h, suffix_v, hidden_v, ids_v, exp_slots_v, gates_v, wgu_h, wdn_h,
    context_h, moe_v,
    pool, tmp_lat, tmp_rope, send_p, arr, fwd, work, keys, q_a, q_b, suf_k, acc, peak, total, out, q_raw,
    wgu, wdn, disp, got, part, rsb, hid, pf, pxs, pxr, ret_s, ret_r, mixw, order_v, order_s,
    ld, disp_ss, disp_rs, page_ss, page_rs, fwd_ss, fwd_rs, sib_ss, sib_rs, x_ss, x_rs, ret_ss, ret_rs, ag_ss, ag_rs,
):
    dp = lax.axis_index("dp")
    mp = lax.axis_index("mp")
    core = lax.rem(dp, 2)
    chip = dp // 2
    y = chip // 8
    z = lax.rem(chip, 8)
    other = 1 - core
    sibling = (chip * 2 + other, mp)

    def shift(k):
        dz = lax.rem(3 * k, 8)
        dy = lax.rem(k // 8 + k, 4)
        return dy, dz

    def to_chip(k):
        dy, dz = shift(k)
        return lax.rem(y + dy, 4) * 8 + lax.rem(z + dz, 8)

    def from_chip(k):
        dy, dz = shift(k)
        return lax.rem(y + 4 - dy, 4) * 8 + lax.rem(z + 8 - dz, 8)

    def x_peer(step):
        return (dp, lax.rem(mp + step, 4))

    barrier = pltpu.get_barrier_semaphore()

    def greet(k, carry):
        pl.semaphore_signal(barrier, inc=1, device_id=(to_chip(k) * 2 + core, mp), device_id_type=MESH)
        return carry

    lax.fori_loop(1, CHIPS, greet, 0)
    pl.semaphore_signal(barrier, inc=1, device_id=sibling, device_id_type=MESH)
    for step in (1, 2, 3):
        pl.semaphore_signal(barrier, inc=1, device_id=x_peer(step), device_id_type=MESH)

    load_pool = pltpu.make_async_copy(pool_h, pool, ld.at[0])
    load_pool.start()
    load_q = pltpu.make_async_copy(queries_h, q_raw, ld.at[1])
    load_q.start()
    load_gu = pltpu.make_async_copy(wgu_h.at[0], wgu, ld.at[2])
    load_gu.start()
    load_dn = pltpu.make_async_copy(wdn_h.at[0], wdn, ld.at[3])
    load_dn.start()

    src = source_v[...]
    src_y = src // 16
    src_z = lax.rem(src // 2, 8)
    res = lax.rem(3 * lax.rem(z + 8 - src_z, 8), 8)
    lap = lax.rem(lax.rem(y + 4 - src_y, 4) + 8 - res, 4)
    lane40 = iota((1, 40), 1)
    rank_key = (lap * 8 + res) * 64 + lane40
    sub = iota((40, 40), 0)
    lane = iota((40, 40), 1)
    key_rows = jnp.broadcast_to(rank_key, (40, 40))
    key_cols = jnp.sum(jnp.where(sub == lane, key_rows, 0), axis=1, keepdims=True)
    rank_col = jnp.sum(jnp.where(key_rows < key_cols, 1, 0), axis=1, keepdims=True)
    src_col = jnp.sum(jnp.where(sub == lane, jnp.broadcast_to(src, (40, 40)), 0), axis=1, keepdims=True)
    hit = iota((40, 128), 1) == rank_col
    seen_col = jnp.where(iota((40, 128), 0) < pages_s[0], 1, 0)
    ordered = jnp.sum(jnp.where(hit, src_col, 0), axis=0, keepdims=True)
    seen = jnp.sum(jnp.where(hit, seen_col, 0), axis=0, keepdims=True)
    row8 = iota((8, 128), 0)
    order_v[...] = jnp.where(row8 == 0, ordered, jnp.where(row8 == 1, seen, 0))
    order_copy = pltpu.make_async_copy(order_v, order_s, ld.at[4])
    order_copy.start()

    ids = ids_v[...]
    exp_slots = exp_slots_v[...]
    target = jnp.where((exp_slots >= 0) & (ids < CHIPS), ids * CAP + exp_slots, -1)
    half_lane = iota((8, 128), 1) // 64
    target = jnp.concatenate([target, target], axis=1)
    target = jnp.where(target >= 0, target * 2 + half_lane, -1)
    gates = jnp.concatenate([gates_v[...], gates_v[...]], axis=1)
    row = iota((256, 128), 0)
    wanted = ((row // 8) * 4 + lax.rem(row, 4)) * 2 + lax.rem(row // 4, 2)
    select = jnp.zeros((256, 128), F32)
    mix = jnp.zeros((256, 128), F32)
    for k in range(8):
        match = wanted == target[k : k + 1, :]
        select = select + jnp.where(match, 1.0, 0.0)
        mix = mix + jnp.where(match, gates[k : k + 1, :], 0.0)
    mixw[...] = mix
    hidden = hidden_v[...]
    halves = jnp.concatenate([hidden[:, :HALF], hidden[:, HALF:]], axis=0)
    picked = dot(select.astype(BF), halves)
    disp[...] = picked.reshape(CHIPS, 8, HALF).astype(BF)

    def disp_copy(k, q):
        return pltpu.make_async_remote_copy(
            src_ref=disp.at[q], dst_ref=got.at[core, k], send_sem=disp_ss.at[k], recv_sem=disp_rs.at[k],
            device_id=(q * 2 + core, mp), device_id_type=MESH,
        )

    def disp_start(k, carry):
        disp_copy(k, to_chip(k)).start()
        return carry

    load_pool.wait()
    perm_row = iota((256, 256), 0)
    perm_col = iota((256, 256), 1)
    perm = jnp.where((lax.rem(perm_row, 16) == perm_col // 16) & (perm_row // 16 == lax.rem(perm_col, 16)), 1.0, 0.0).astype(BF)
    for g in range(4):
        lat_rows = []
        rope_rows = []
        for t in range(16):
            start = t * ENT
            lat_rows.append(pool[g * 16 : g * 16 + 16, start : start + KVL])
            rope = pool[g * 16 : g * 16 + 16, start + KVL : start + ENT]
            rope_rows.append(jnp.concatenate([rope, rope], axis=1))
        lat = dot(perm, jnp.concatenate(lat_rows, axis=0)).astype(BF)
        rope = dot(perm, jnp.concatenate(rope_rows, axis=0)).astype(BF)
        for p in range(16):
            for c in range(4):
                tmp_lat[g * 16 + p, c * 16 : c * 16 + 16, :] = lat[p * 16 : p * 16 + 16, c * 128 : c * 128 + 128]
            tmp_rope[g * 16 + p] = rope[p * 16 : p * 16 + 16, :]

    low_lane = iota((16, 128), 1) < 64

    def page_copy(k, q):
        return pltpu.make_async_remote_copy(
            src_ref=send_p.at[q], dst_ref=arr.at[chip], send_sem=page_ss.at[k], recv_sem=page_rs.at[k],
            device_id=(q * 2 + core, mp), device_id_type=MESH,
        )

    def page_fill(q):
        first = slots_s[0, 2 * q]
        second = slots_s[0, 2 * q + 1]
        send_p[q, 0:64, :] = tmp_lat[first]
        send_p[q, 64:80, :] = jnp.where(low_lane, tmp_rope[first], tmp_rope[second])
        send_p[q, 80:144, :] = tmp_lat[second]

    def fill(q, carry):
        page_fill(q)
        return carry

    def page_start(k, carry):
        page_copy(k, to_chip(k)).start()
        return carry

    lax.fori_loop(0, CHIPS, fill, 0)

    load_q.wait()
    zeros = jnp.zeros((64, 64), BF)
    for h in range(HEADS):
        rows = slice(h * 64, h * 64 + 64)
        start = h * ENT
        lat = q_raw[:, start : start + KVL]
        rope = q_raw[:, start + KVL : start + ENT]
        q_a[rows, 0:KVL] = lat
        q_a[rows, KVL : KVL + 128] = jnp.concatenate([rope, zeros], axis=1)
        q_b[rows, 0:128] = jnp.concatenate([zeros, rope], axis=1)
        q_b[rows, 128 : 128 + KVL] = lat

    suf_k[:, 0:KVL] = suffix_v[:, 0:KVL]
    suf_k[:, KVL : KVL + 128] = jnp.concatenate([suffix_v[:, KVL:ENT], zeros], axis=1)

    def suffix_block(b, carry):
        rows = pl.ds(pl.multiple_of(b * BLK, BLK), BLK)
        s = dot_nt(q_a[rows, :], suf_k[...]) * GAIN
        token = lax.rem(iota((BLK, 64), 0), 64)
        s = jnp.where(iota((BLK, 64), 1) <= token, s, LOW)
        top = jnp.max(s, axis=1, keepdims=True)
        w = jnp.exp2(s - top)
        peak[rows, :] = jnp.broadcast_to(top, (BLK, 128))
        total[rows, :] = jnp.concatenate([w, jnp.zeros((BLK, 64), F32)], axis=1)
        acc[rows, :] = dot(w.astype(BF), suf_k[:, 0:KVL])
        return carry

    lax.fori_loop(0, ROWS // BLK, suffix_block, 0)

    pl.semaphore_wait(barrier, CHIPS + 3)
    lax.fori_loop(1, PRE, page_start, 0)
    lax.fori_loop(1, CHIPS, disp_start, 0)
    lax.fori_loop(PRE, CHIPS, page_start, 0)
    got[core, 0] = disp[chip]
    arr[chip] = send_p[chip]

    def forward_copy(k, q):
        return pltpu.make_async_remote_copy(
            src_ref=arr.at[q, pl.ds(pl.multiple_of(64 * other, 16), 80)], dst_ref=fwd.at[q],
            send_sem=fwd_ss.at[k], recv_sem=fwd_rs.at[k], device_id=sibling, device_id_type=MESH,
        )

    def arrive(k, carry):
        q = from_chip(k)
        page_copy(k, q).wait_recv()
        forward_copy(k, q).start()
        return carry

    def arrivals(stage):
        if stage == 0:
            forward_copy(0, chip).start()
            lax.fori_loop(1, FIRST, arrive, 0)
        else:
            lax.fori_loop(FIRST + STEP * (stage - 1), FIRST + STEP * stage, arrive, 0)

    def both_halves(tile):
        wide = tile.astype(F32)
        turned = pltpu.roll(wide, 64, 1)
        keep = (iota((16, 128), 1) // 64) == core
        return jnp.where(keep, wide, turned).astype(BF)

    def settle(k, carry):
        q = from_chip(k)
        forward_copy(k, q).wait_recv()
        work[0, q, 0:64, :] = arr[q, pl.ds(pl.multiple_of(80 * core, 16), 64), :]
        work[0, q, 64:80, :] = both_halves(arr[q, 64:80, :])
        work[1, q, 0:64, :] = fwd[q, pl.ds(pl.multiple_of(16 * core, 16), 64), :]
        work[1, q, 64:80, :] = both_halves(fwd[q, pl.ds(pl.multiple_of(64 * other, 16), 16), :])
        return carry

    mine = pl.ds(pl.multiple_of(mp * 64, 64), 64)

    def near_copy(ch, step):
        way = 0 if step == 1 else 1
        return pltpu.make_async_remote_copy(
            src_ref=keys.at[ch, mine], dst_ref=keys.at[ch, mine], send_sem=ag_ss.at[ch, way], recv_sem=ag_rs.at[ch, way],
            device_id=x_peer(step), device_id_type=MESH,
        )

    def far_copy(ch, step):
        way = 2 if step == 1 else 3
        owner = lax.rem(mp + 4 - step, 4)
        begin = owner * 64 + (0 if step == 1 else 32)
        rows = pl.ds(pl.multiple_of(begin, 32), 32)
        return pltpu.make_async_remote_copy(
            src_ref=keys.at[ch, rows], dst_ref=keys.at[ch, rows], send_sem=ag_ss.at[ch, way], recv_sem=ag_rs.at[ch, way],
            device_id=x_peer(step), device_id_type=MESH,
        )

    def gather_chunk(ch):
        if ch == 0:
            lax.fori_loop(0, FIRST, settle, 0)
        else:
            lax.fori_loop(FIRST + STEP * (ch - 1), FIRST + STEP * ch, settle, 0)

        def pick(i, carry):
            a = jnp.clip(order_s[0, ch * 8 + i], 0, 63)
            b = jnp.clip(order_s[0, ch * 8 + 4 + i], 0, 63)
            rel_a = lax.rem(lax.rem(a, 2) + core, 2)
            rel_b = lax.rem(lax.rem(b, 2) + core, 2)
            page_a = work[rel_a, a // 2]
            page_b = work[rel_b, b // 2]
            rows = pl.ds(pl.multiple_of(mp * 64 + i * 16, 16), 16)
            for c in range(4):
                keys[ch, rows, c * 128 : c * 128 + 128] = page_a[c * 16 : c * 16 + 16, :]
                keys[ch, rows, 640 + c * 128 : 640 + c * 128 + 128] = page_b[c * 16 : c * 16 + 16, :]
            keys[ch, rows, 512:640] = jnp.where(low_lane, page_a[64:80, :], page_b[64:80, :])
            return carry

        lax.fori_loop(0, 4, pick, 0)
        near_copy(ch, 1).start()
        near_copy(ch, 3).start()

    def relay_chunk(ch):
        near_copy(ch, 1).wait_recv()
        far_copy(ch, 1).start()
        near_copy(ch, 3).wait_recv()
        far_copy(ch, 3).start()

    def store_copy(b):
        span = BLK // 64 * KVL
        cols = slice(b * span, b * span + span)
        return pltpu.make_async_copy(out.at[:, cols], context_h.at[:, cols], ld.at[5 + b])

    def finish(b):
        for h in range(b * BLK // 64, (b + 1) * BLK // 64):
            rows = slice(h * 64, h * 64 + 64)
            whole = jnp.sum(total[rows, :], axis=1, keepdims=True)
            out[:, h * KVL : h * KVL + KVL] = (acc[rows, :] / whole).astype(BF)
        store_copy(b).start()

    def attend_chunk(ch):
        far_copy(ch, 1).wait_recv()
        far_copy(ch, 3).wait_recv()
        page_lane = lax.rem(iota((1, KEYS), 1) // 16, 4)

        def bias(base):
            value = jnp.zeros((1, KEYS), F32)
            for i in range(4):
                shown = order_s[1, ch * 8 + base + i].astype(F32)
                value = jnp.where(page_lane == i, (shown - 1.0) * -LOW, value)
            return value

        bias_a = bias(0)
        bias_b = bias(4)

        def scores(b):
            rows = slice(b * BLK, b * BLK + BLK)
            s_a = dot_nt(q_a[rows, :], keys[ch, :, 0:640]) * GAIN + bias_a
            s_b = dot_nt(q_b[rows, :], keys[ch, :, 512:1152]) * GAIN + bias_b
            return s_a, s_b

        def absorb(b, s_a, s_b):
            rows = slice(b * BLK, b * BLK + BLK)
            old = peak[rows, :]
            top = jnp.maximum(s_a, s_b)
            top = jnp.max(jnp.maximum(top[:, 0:128], top[:, 128:256]), axis=1, keepdims=True)
            top = jnp.maximum(jnp.broadcast_to(top, (BLK, 128)), old)
            factor = jnp.exp2(old - top)
            top2 = jnp.concatenate([top, top], axis=1)
            w_a = jnp.exp2(s_a - top2)
            w_b = jnp.exp2(s_b - top2)
            both = w_a + w_b
            peak[rows, :] = top
            total[rows, :] = total[rows, :] * factor + both[:, 0:128] + both[:, 128:256]
            w = jnp.concatenate([w_a.astype(BF), w_b.astype(BF)], axis=1)
            v = jnp.concatenate([keys[ch, :, 0:KVL], keys[ch, :, 640 : 640 + KVL]], axis=0)
            acc[rows, :] = acc[rows, :] * jnp.concatenate([factor] * 4, axis=1) + dot(w, v)

        blocks = ROWS // BLK
        now = scores(0)
        for b in range(blocks):
            later = scores(b + 1) if b + 1 < blocks else None
            absorb(b, *now)
            now = later
            if ch == CHUNKS - 1:
                finish(b)

    half = CHIPS // 2

    def got_copy(k):
        return pltpu.make_async_remote_copy(
            src_ref=got.at[core, k], dst_ref=got.at[core, k], send_sem=sib_ss.at[k], recv_sem=sib_rs.at[k],
            device_id=sibling, device_id_type=MESH,
        )

    def disp_arrive(k, carry):
        disp_copy(k, to_chip(k)).wait_recv()
        got_copy(k).start()
        return carry

    def got_wait(k, carry):
        got_copy(k).wait_recv()
        return carry

    def sum_copy(n, step):
        there = lax.rem(mp + step, 4)
        return pltpu.make_async_remote_copy(
            src_ref=part.at[n, pl.ds(pl.multiple_of(there * 32, 32), 32)], dst_ref=rsb.at[n, mp],
            send_sem=x_ss.at[n, step - 1], recv_sem=x_rs.at[n, step - 1], device_id=x_peer(step), device_id_type=MESH,
        )

    mine32 = pl.ds(pl.multiple_of(mp * 32, 32), 32)

    def hid_copy(n, step):
        return pltpu.make_async_remote_copy(
            src_ref=hid.at[n, mine32], dst_ref=hid.at[n, mine32],
            send_sem=x_ss.at[n, step + 2], recv_sem=x_rs.at[n, step + 2], device_id=x_peer(step), device_id_type=MESH,
        )

    def part_copy(n):
        return pltpu.make_async_remote_copy(
            src_ref=pxs.at[n], dst_ref=pxr.at[n], send_sem=sib_ss.at[CHIPS + n], recv_sem=sib_rs.at[CHIPS + n],
            device_id=sibling, device_id_type=MESH,
        )

    def ret_copy(k):
        return pltpu.make_async_remote_copy(
            src_ref=ret_s.at[k], dst_ref=ret_r.at[chip], send_sem=ret_ss.at[k], recv_sem=ret_rs.at[k],
            device_id=(from_chip(k) * 2 + core, mp), device_id_type=MESH,
        )

    def expert_up(n):
        if n == 0:
            got_copy(0).start()
        lax.fori_loop(max(1, n * half), n * half + half, disp_arrive, 0)
        if n == 0:
            load_gu.wait()
        lax.fori_loop(n * half, n * half + half, got_wait, 0)
        rows = jnp.concatenate([got[0, n * half : n * half + half], got[1, n * half : n * half + half]], axis=0)
        rows = rows.astype(F32).reshape(256, HALF).astype(BF)
        pr = iota((128, 256), 0)
        pc = iota((128, 256), 1)
        same = (pr // 4 == pc // 8) & (lax.rem(pr, 4) == lax.rem(pc, 4))
        left = dot(jnp.where(same & (lax.rem(pc // 4, 2) == 0), 1.0, 0.0).astype(BF), rows).astype(BF)
        right = dot(jnp.where(same & (lax.rem(pc // 4, 2) == 1), 1.0, 0.0).astype(BF), rows).astype(BF)
        part[n] = (dot(left, wgu[0:HALF, :]) + dot(right, wgu[HALF : 2 * HALF, :])).astype(BF)
        for step in (2, 1, 3):
            sum_copy(n, step).start()
        rsb[n, mp] = part[n, mine32, :]

    def expert_act(n):
        for step in (1, 2, 3):
            sum_copy(n, step).wait_recv()
        pre = rsb[n, 0].astype(F32) + rsb[n, 1].astype(F32) + rsb[n, 2].astype(F32) + rsb[n, 3].astype(F32)
        gate = pre[:, 0:512]
        hid[n, mine32, :] = (gate / (1.0 + jnp.exp(-gate)) * pre[:, 512:1024]).astype(BF)
        for step in (2, 1, 3):
            hid_copy(n, step).start()

    def expert_down(n):
        if n == 0:
            load_dn.wait()
        for step in (1, 2, 3):
            hid_copy(n, step).wait_recv()
        dr = iota((256, 128), 0)
        dc = iota((256, 128), 1)
        twice = jnp.where((dr // 8 == dc // 4) & (lax.rem(dr, 4) == lax.rem(dc, 4)), 1.0, 0.0).astype(BF)
        doubled = dot(twice, hid[n]).astype(BF)
        is_left = lax.rem(iota((256, HALF), 0) // 4, 2) == 0
        both = jnp.where(is_left, dot(doubled, wdn[:, 0:HALF]), dot(doubled, wdn[:, HALF : 2 * HALF]))
        pf[n] = both.reshape(2, 128, HALF)
        pxs[n] = pf[n, other].astype(BF)
        part_copy(n).start()

    def ret_start(k, carry):
        ret_copy(k).start()
        return carry

    def expert_back(n):
        part_copy(n).wait_recv()
        rows = slice(n * half, n * half + half)
        ret_s[rows] = (pf[n, core] + pxr[n].astype(F32)).reshape(half, 8, HALF).astype(BF)
        lax.fori_loop(max(1, n * half), n * half + half, ret_start, 0)
        if n == 0:
            ret_r[chip] = ret_s[0]

    def expert_mix():
        def ret_wait(k, carry):
            ret_copy(k).wait_recv()
            return carry

        lax.fori_loop(1, CHIPS, ret_wait, 0)
        rows256 = ret_r[...].astype(F32).reshape(256, HALF).astype(BF)
        weights = mixw[...]
        high = weights.astype(BF)
        low = (weights - high.astype(F32)).astype(BF)
        dims = (((0,), (0,)), ((), ()))
        mixed = lax.dot_general(high, rows256, dims, preferred_element_type=F32) + lax.dot_general(
            low, rows256, dims, preferred_element_type=F32
        )
        moe_v[:, 0:HALF] = mixed[0:64].astype(BF)
        moe_v[:, HALF : 2 * HALF] = mixed[64:128].astype(BF)


    order_copy.wait()
    expert_up(0)
    expert_up(1)
    expert_act(0)
    expert_act(1)
    arrivals(0)
    gather_chunk(0)
    arrivals(1)
    gather_chunk(1)
    expert_down(0)
    arrivals(2)
    gather_chunk(2)
    expert_down(1)
    relay_chunk(0)
    arrivals(3)
    gather_chunk(3)
    relay_chunk(1)
    arrivals(4)
    gather_chunk(4)
    relay_chunk(2)
    expert_back(0)
    expert_back(1)
    attend_chunk(0)
    relay_chunk(3)
    attend_chunk(1)
    relay_chunk(4)
    attend_chunk(2)
    attend_chunk(3)
    attend_chunk(4)
    expert_mix()

    def sent(k, carry):
        disp_copy(k, to_chip(k)).wait_send()
        page_copy(k, to_chip(k)).wait_send()
        forward_copy(k, from_chip(k)).wait_send()
        ret_copy(k).wait_send()
        got_copy(k).wait_send()
        return carry

    lax.fori_loop(1, CHIPS, sent, 0)
    forward_copy(0, chip).wait_send()
    got_copy(0).wait_send()
    for n in range(2):
        part_copy(n).wait_send()
        for step in (1, 2, 3):
            sum_copy(n, step).wait_send()
            hid_copy(n, step).wait_send()
    for ch in range(CHUNKS):
        for step in (1, 3):
            near_copy(ch, step).wait_send()
            far_copy(ch, step).wait_send()
    for b in range(ROWS // BLK):
        store_copy(b).wait()


def body(
    pool, send_slots, page_source, prefix_pages, queries, suffix_kv, hidden_in,
    expert_ids, expert_slots, gate_weights, w_gate_up, w_down,
):
    any_spec = pl.BlockSpec(memory_space=pl.ANY)
    vmem = pl.BlockSpec(memory_space=pltpu.VMEM)
    smem = pl.BlockSpec(memory_space=pltpu.SMEM)
    dma = pltpu.SemaphoreType.DMA
    scratch = [
        pltpu.VMEM((64, 9216), BF),
        pltpu.VMEM((64, 64, 128), BF),
        pltpu.VMEM((64, 16, 128), BF),
        pltpu.VMEM((CHIPS, 144, 128), BF),
        pltpu.VMEM((CHIPS, 144, 128), BF),
        pltpu.VMEM((CHIPS, 80, 128), BF),
        pltpu.VMEM((2, CHIPS, 80, 128), BF),
        pltpu.VMEM((CHUNKS, KEYS, WIDE), BF),
        pltpu.VMEM((ROWS, 640), BF),
        pltpu.VMEM((ROWS, 640), BF),
        pltpu.VMEM((64, 640), BF),
        pltpu.VMEM((ROWS, KVL), F32),
        pltpu.VMEM((ROWS, 128), F32),
        pltpu.VMEM((ROWS, 128), F32),
        pltpu.VMEM((64, HEADS * KVL), BF),
        pltpu.VMEM((64, HEADS * ENT), BF),
        pltpu.VMEM((2 * HALF, 1024), BF),
        pltpu.VMEM((512, 2 * HALF), BF),
        pltpu.VMEM((CHIPS, 8, HALF), BF),
        pltpu.VMEM((2, CHIPS, 8, HALF), BF),
        pltpu.VMEM((2, 128, 1024), BF),
        pltpu.VMEM((2, 4, 32, 1024), BF),
        pltpu.VMEM((2, 128, 512), BF),
        pltpu.VMEM((2, 2, 128, HALF), F32),
        pltpu.VMEM((2, 128, HALF), BF),
        pltpu.VMEM((2, 128, HALF), BF),
        pltpu.VMEM((CHIPS, 8, HALF), BF),
        pltpu.VMEM((CHIPS, 8, HALF), BF),
        pltpu.VMEM((256, 128), F32),
        pltpu.VMEM((8, 128), I32),
        pltpu.SMEM((8, 128), I32),
        dma((9,)),
        dma((CHIPS,)), dma((CHIPS,)),
        dma((CHIPS,)), dma((CHIPS,)),
        dma((CHIPS,)), dma((CHIPS,)),
        dma((CHIPS + 2,)), dma((CHIPS + 2,)),
        dma((2, 6)), dma((2, 6)),
        dma((CHIPS,)), dma((CHIPS,)),
        dma((CHUNKS, 4)), dma((CHUNKS, 4)),
    ]
    context, moe_out = pl.pallas_call(
        kernel,
        out_shape=(
            jax.ShapeDtypeStruct((64, HEADS * KVL), BF),
            jax.ShapeDtypeStruct((64, 2 * HALF), BF),
        ),
        in_specs=[any_spec, smem, vmem, smem, any_spec, vmem, vmem, vmem, vmem, vmem, any_spec, any_spec],
        out_specs=(any_spec, vmem),
        scratch_shapes=scratch,
        compiler_params=pltpu.CompilerParams(
            collective_id=0, has_side_effects=True, vmem_limit_bytes=56 * 2**20
        ),
        name="prefill",
    )(
        pool, send_slots, page_source, prefix_pages, queries, suffix_kv, hidden_in,
        expert_ids.T, expert_slots.T, gate_weights.T, w_gate_up, w_down,
    )
    return context, moe_out


def solution(mesh):
    return jax.shard_map(
        body,
        mesh=mesh,
        in_specs=(
            P("dp", "mp"),
            P("dp", None),
            P("dp", None),
            P("dp"),
            P("dp", "mp"),
            P("dp", None),
            P("dp", "mp"),
            P("dp", None),
            P("dp", None),
            P("dp", None),
            P("dp", "mp", None),
            P("dp", None, "mp"),
        ),
        out_specs=(P("dp", "mp"), P("dp", "mp")),
        check_vma=False,
    )
```

```python
import functools

import jax
import jax.numpy as jnp
from jax import lax
from jax.experimental import pallas as pl
from jax.experimental.pallas import tpu as pltpu
from jax.sharding import PartitionSpec as P

MESH = pl.DeviceIdType.MESH
BF = jnp.bfloat16
F32 = jnp.float32
I32 = jnp.int32

KVL = 512
ENT = 576
PAGE = 64
CAP = 4
CHIPS = 32
HALF = 896
CHUNKS = 5
KEYS = 256
WIDE = 1152
HEADS = 32
ROWS = 2048
BLK = 512
LOW = -1e30
GAIN = 192 ** (-0.5) * 1.4426950408889634
FIRST = 16
STEP = 4
PRE = 1


def dot(a, b):
    return jnp.dot(a, b, preferred_element_type=F32)


def dot_nt(a, b):
    return lax.dot_general(a, b, (((1,), (1,)), ((), ())), preferred_element_type=F32)


def iota(shape, axis):
    return lax.broadcasted_iota(I32, shape, axis)


def kernel(
    pool_h, slots_s, source_v, pages_s, queries_h, suffix_v, hidden_v, ids_v, exp_slots_v, gates_v, wgu_h, wdn_h,
    context_h, moe_v,
    pool, tmp_lat, tmp_rope, send_p, arr, fwd, work, keys, q_a, q_b, suf_k, acc, peak, total, out, q_raw,
    wgu, wdn, disp, got, part, rsb, hid, pf, pxs, pxr, ret_s, ret_r, mixw, order_v, order_s,
    ld, disp_ss, disp_rs, page_ss, page_rs, fwd_ss, fwd_rs, sib_ss, sib_rs, x_ss, x_rs, ret_ss, ret_rs, ag_ss, ag_rs,
):
    dp = lax.axis_index("dp")
    mp = lax.axis_index("mp")
    core = lax.rem(dp, 2)
    chip = dp // 2
    y = chip // 8
    z = lax.rem(chip, 8)
    other = 1 - core
    sibling = (chip * 2 + other, mp)

    def shift(k):
        dz = lax.rem(3 * k, 8)
        dy = lax.rem(k // 8 + k, 4)
        return dy, dz

    def to_chip(k):
        dy, dz = shift(k)
        return lax.rem(y + dy, 4) * 8 + lax.rem(z + dz, 8)

    def from_chip(k):
        dy, dz = shift(k)
        return lax.rem(y + 4 - dy, 4) * 8 + lax.rem(z + 8 - dz, 8)

    def x_peer(step):
        return (dp, lax.rem(mp + step, 4))

    barrier = pltpu.get_barrier_semaphore()

    def greet(k, carry):
        pl.semaphore_signal(barrier, inc=1, device_id=(to_chip(k) * 2 + core, mp), device_id_type=MESH)
        return carry

    lax.fori_loop(1, CHIPS, greet, 0, unroll=True)
    pl.semaphore_signal(barrier, inc=1, device_id=sibling, device_id_type=MESH)
    for step in (1, 2, 3):
        pl.semaphore_signal(barrier, inc=1, device_id=x_peer(step), device_id_type=MESH)

    load_pool = pltpu.make_async_copy(pool_h, pool, ld.at[0])
    load_pool.start()
    load_q = pltpu.make_async_copy(queries_h, q_raw, ld.at[1])
    load_q.start()
    load_gu = pltpu.make_async_copy(wgu_h.at[0], wgu, ld.at[2])
    load_gu.start()
    load_dn = pltpu.make_async_copy(wdn_h.at[0], wdn, ld.at[3])
    load_dn.start()

    src = source_v[...]
    src_y = src // 16
    src_z = lax.rem(src // 2, 8)
    res = lax.rem(3 * lax.rem(z + 8 - src_z, 8), 8)
    lap = lax.rem(lax.rem(y + 4 - src_y, 4) + 8 - res, 4)
    lane40 = iota((1, 40), 1)
    rank_key = (lap * 8 + res) * 64 + lane40
    sub = iota((40, 40), 0)
    lane = iota((40, 40), 1)
    key_rows = jnp.broadcast_to(rank_key, (40, 40))
    key_cols = jnp.sum(jnp.where(sub == lane, key_rows, 0), axis=1, keepdims=True)
    rank_col = jnp.sum(jnp.where(key_rows < key_cols, 1, 0), axis=1, keepdims=True)
    src_col = jnp.sum(jnp.where(sub == lane, jnp.broadcast_to(src, (40, 40)), 0), axis=1, keepdims=True)
    hit = iota((40, 128), 1) == rank_col
    seen_col = jnp.where(iota((40, 128), 0) < pages_s[0], 1, 0)
    ordered = jnp.sum(jnp.where(hit, src_col, 0), axis=0, keepdims=True)
    seen = jnp.sum(jnp.where(hit, seen_col, 0), axis=0, keepdims=True)
    row8 = iota((8, 128), 0)
    order_v[...] = jnp.where(row8 == 0, ordered, jnp.where(row8 == 1, seen, 0))
    order_copy = pltpu.make_async_copy(order_v, order_s, ld.at[4])
    order_copy.start()

    ids = ids_v[...]
    exp_slots = exp_slots_v[...]
    target = jnp.where((exp_slots >= 0) & (ids < CHIPS), ids * CAP + exp_slots, -1)
    half_lane = iota((8, 128), 1) // 64
    target = jnp.concatenate([target, target], axis=1)
    target = jnp.where(target >= 0, target * 2 + half_lane, -1)
    gates = jnp.concatenate([gates_v[...], gates_v[...]], axis=1)
    row = iota((256, 128), 0)
    wanted = ((row // 8) * 4 + lax.rem(row, 4)) * 2 + lax.rem(row // 4, 2)
    select = jnp.zeros((256, 128), F32)
    mix = jnp.zeros((256, 128), F32)
    for k in range(8):
        match = wanted == target[k : k + 1, :]
        select = select + jnp.where(match, 1.0, 0.0)
        mix = mix + jnp.where(match, gates[k : k + 1, :], 0.0)
    mixw[...] = mix
    hidden = hidden_v[...]
    halves = jnp.concatenate([hidden[:, :HALF], hidden[:, HALF:]], axis=0)
    picked = dot(select.astype(BF), halves)
    disp[...] = picked.reshape(CHIPS, 8, HALF).astype(BF)

    def disp_copy(k, q):
        return pltpu.make_async_remote_copy(
            src_ref=disp.at[q], dst_ref=got.at[core, k], send_sem=disp_ss.at[k], recv_sem=disp_rs.at[k],
            device_id=(q * 2 + core, mp), device_id_type=MESH,
        )

    def disp_start(k, carry):
        disp_copy(k, to_chip(k)).start()
        return carry

    load_pool.wait()
    perm_row = iota((256, 256), 0)
    perm_col = iota((256, 256), 1)
    perm = jnp.where((lax.rem(perm_row, 16) == perm_col // 16) & (perm_row // 16 == lax.rem(perm_col, 16)), 1.0, 0.0).astype(BF)
    for g in range(4):
        lat_rows = []
        rope_rows = []
        for t in range(16):
            start = t * ENT
            lat_rows.append(pool[g * 16 : g * 16 + 16, start : start + KVL])
            rope = pool[g * 16 : g * 16 + 16, start + KVL : start + ENT]
            rope_rows.append(jnp.concatenate([rope, rope], axis=1))
        lat = dot(perm, jnp.concatenate(lat_rows, axis=0)).astype(BF)
        rope = dot(perm, jnp.concatenate(rope_rows, axis=0)).astype(BF)
        for p in range(16):
            for c in range(4):
                tmp_lat[g * 16 + p, c * 16 : c * 16 + 16, :] = lat[p * 16 : p * 16 + 16, c * 128 : c * 128 + 128]
            tmp_rope[g * 16 + p] = rope[p * 16 : p * 16 + 16, :]

    low_lane = iota((16, 128), 1) < 64

    def page_copy(k, q):
        return pltpu.make_async_remote_copy(
            src_ref=send_p.at[q], dst_ref=arr.at[chip], send_sem=page_ss.at[k], recv_sem=page_rs.at[k],
            device_id=(q * 2 + core, mp), device_id_type=MESH,
        )

    def page_fill(q):
        first = slots_s[0, 2 * q]
        second = slots_s[0, 2 * q + 1]
        send_p[q, 0:64, :] = tmp_lat[first]
        send_p[q, 64:80, :] = jnp.where(low_lane, tmp_rope[first], tmp_rope[second])
        send_p[q, 80:144, :] = tmp_lat[second]

    def fill(q, carry):
        page_fill(q)
        return carry

    def page_start(k, carry):
        page_copy(k, to_chip(k)).start()
        return carry

    lax.fori_loop(0, CHIPS, fill, 0)

    load_q.wait()
    zeros = jnp.zeros((64, 64), BF)
    for h in range(HEADS):
        rows = slice(h * 64, h * 64 + 64)
        start = h * ENT
        lat = q_raw[:, start : start + KVL]
        rope = q_raw[:, start + KVL : start + ENT]
        q_a[rows, 0:KVL] = lat
        q_a[rows, KVL : KVL + 128] = jnp.concatenate([rope, zeros], axis=1)
        q_b[rows, 0:128] = jnp.concatenate([zeros, rope], axis=1)
        q_b[rows, 128 : 128 + KVL] = lat

    suf_k[:, 0:KVL] = suffix_v[:, 0:KVL]
    suf_k[:, KVL : KVL + 128] = jnp.concatenate([suffix_v[:, KVL:ENT], zeros], axis=1)

    def suffix_block(b, carry):
        rows = pl.ds(pl.multiple_of(b * BLK, BLK), BLK)
        s = dot_nt(q_a[rows, :], suf_k[...]) * GAIN
        token = lax.rem(iota((BLK, 64), 0), 64)
        s = jnp.where(iota((BLK, 64), 1) <= token, s, LOW)
        top = jnp.max(s, axis=1, keepdims=True)
        w = jnp.exp2(s - top)
        peak[rows, :] = jnp.broadcast_to(top, (BLK, 128))
        total[rows, :] = jnp.concatenate([w, jnp.zeros((BLK, 64), F32)], axis=1)
        acc[rows, :] = dot(w.astype(BF), suf_k[:, 0:KVL])
        return carry

    lax.fori_loop(0, ROWS // BLK, suffix_block, 0)

    pl.semaphore_wait(barrier, CHIPS + 3)
    lax.fori_loop(1, PRE, page_start, 0, unroll=True)
    lax.fori_loop(1, CHIPS, disp_start, 0, unroll=True)
    lax.fori_loop(PRE, CHIPS, page_start, 0, unroll=True)
    got[core, 0] = disp[chip]
    arr[chip] = send_p[chip]

    def forward_copy(k, q):
        return pltpu.make_async_remote_copy(
            src_ref=arr.at[q, pl.ds(pl.multiple_of(64 * other, 16), 80)], dst_ref=fwd.at[q],
            send_sem=fwd_ss.at[k], recv_sem=fwd_rs.at[k], device_id=sibling, device_id_type=MESH,
        )

    def arrive(k, carry):
        q = from_chip(k)
        page_copy(k, q).wait_recv()
        forward_copy(k, q).start()
        return carry

    def arrivals(stage):
        if stage == 0:
            forward_copy(0, chip).start()
            lax.fori_loop(1, FIRST, arrive, 0)
        else:
            lax.fori_loop(FIRST + STEP * (stage - 1), FIRST + STEP * stage, arrive, 0)

    def both_halves(tile):
        wide = tile.astype(F32)
        turned = pltpu.roll(wide, 64, 1)
        keep = (iota((16, 128), 1) // 64) == core
        return jnp.where(keep, wide, turned).astype(BF)

    def settle(k, carry):
        q = from_chip(k)
        forward_copy(k, q).wait_recv()
        work[0, q, 0:64, :] = arr[q, pl.ds(pl.multiple_of(80 * core, 16), 64), :]
        work[0, q, 64:80, :] = both_halves(arr[q, 64:80, :])
        work[1, q, 0:64, :] = fwd[q, pl.ds(pl.multiple_of(16 * core, 16), 64), :]
        work[1, q, 64:80, :] = both_halves(fwd[q, pl.ds(pl.multiple_of(64 * other, 16), 16), :])
        return carry

    mine = pl.ds(pl.multiple_of(mp * 64, 64), 64)

    def near_copy(ch, step):
        way = 0 if step == 1 else 1
        return pltpu.make_async_remote_copy(
            src_ref=keys.at[ch, mine], dst_ref=keys.at[ch, mine], send_sem=ag_ss.at[ch, way], recv_sem=ag_rs.at[ch, way],
            device_id=x_peer(step), device_id_type=MESH,
        )

    def far_copy(ch, step):
        way = 2 if step == 1 else 3
        owner = lax.rem(mp + 4 - step, 4)
        begin = owner * 64 + (0 if step == 1 else 32)
        rows = pl.ds(pl.multiple_of(begin, 32), 32)
        return pltpu.make_async_remote_copy(
            src_ref=keys.at[ch, rows], dst_ref=keys.at[ch, rows], send_sem=ag_ss.at[ch, way], recv_sem=ag_rs.at[ch, way],
            device_id=x_peer(step), device_id_type=MESH,
        )

    def gather_chunk(ch):
        if ch == 0:
            lax.fori_loop(0, FIRST, settle, 0)
        else:
            lax.fori_loop(FIRST + STEP * (ch - 1), FIRST + STEP * ch, settle, 0)

        def pick(i, carry):
            a = jnp.clip(order_s[0, ch * 8 + i], 0, 63)
            b = jnp.clip(order_s[0, ch * 8 + 4 + i], 0, 63)
            rel_a = lax.rem(lax.rem(a, 2) + core, 2)
            rel_b = lax.rem(lax.rem(b, 2) + core, 2)
            page_a = work[rel_a, a // 2]
            page_b = work[rel_b, b // 2]
            rows = pl.ds(pl.multiple_of(mp * 64 + i * 16, 16), 16)
            for c in range(4):
                keys[ch, rows, c * 128 : c * 128 + 128] = page_a[c * 16 : c * 16 + 16, :]
                keys[ch, rows, 640 + c * 128 : 640 + c * 128 + 128] = page_b[c * 16 : c * 16 + 16, :]
            keys[ch, rows, 512:640] = jnp.where(low_lane, page_a[64:80, :], page_b[64:80, :])
            return carry

        lax.fori_loop(0, 4, pick, 0)
        near_copy(ch, 1).start()
        near_copy(ch, 3).start()

    def relay_chunk(ch):
        near_copy(ch, 1).wait_recv()
        far_copy(ch, 1).start()
        near_copy(ch, 3).wait_recv()
        far_copy(ch, 3).start()

    def store_copy(b):
        span = BLK // 64 * KVL
        cols = slice(b * span, b * span + span)
        return pltpu.make_async_copy(out.at[:, cols], context_h.at[:, cols], ld.at[5 + b])

    def finish(b):
        for h in range(b * BLK // 64, (b + 1) * BLK // 64):
            rows = slice(h * 64, h * 64 + 64)
            whole = jnp.sum(total[rows, :], axis=1, keepdims=True)
            out[:, h * KVL : h * KVL + KVL] = (acc[rows, :] / whole).astype(BF)
        store_copy(b).start()

    def attend_chunk(ch):
        far_copy(ch, 1).wait_recv()
        far_copy(ch, 3).wait_recv()
        page_lane = lax.rem(iota((1, KEYS), 1) // 16, 4)

        def bias(base):
            value = jnp.zeros((1, KEYS), F32)
            for i in range(4):
                shown = order_s[1, ch * 8 + base + i].astype(F32)
                value = jnp.where(page_lane == i, (shown - 1.0) * -LOW, value)
            return value

        bias_a = bias(0)
        bias_b = bias(4)

        def scores(b):
            rows = slice(b * BLK, b * BLK + BLK)
            s_a = dot_nt(q_a[rows, :], keys[ch, :, 0:640]) * GAIN + bias_a
            s_b = dot_nt(q_b[rows, :], keys[ch, :, 512:1152]) * GAIN + bias_b
            return s_a, s_b

        def absorb(b, s_a, s_b):
            rows = slice(b * BLK, b * BLK + BLK)
            old = peak[rows, :]
            top = jnp.maximum(s_a, s_b)
            top = jnp.max(jnp.maximum(top[:, 0:128], top[:, 128:256]), axis=1, keepdims=True)
            top = jnp.maximum(jnp.broadcast_to(top, (BLK, 128)), old)
            factor = jnp.exp2(old - top)
            top2 = jnp.concatenate([top, top], axis=1)
            w_a = jnp.exp2(s_a - top2)
            w_b = jnp.exp2(s_b - top2)
            both = w_a + w_b
            peak[rows, :] = top
            total[rows, :] = total[rows, :] * factor + both[:, 0:128] + both[:, 128:256]
            w = jnp.concatenate([w_a.astype(BF), w_b.astype(BF)], axis=1)
            v = jnp.concatenate([keys[ch, :, 0:KVL], keys[ch, :, 640 : 640 + KVL]], axis=0)
            acc[rows, :] = acc[rows, :] * jnp.concatenate([factor] * 4, axis=1) + dot(w, v)

        blocks = ROWS // BLK
        now = scores(0)
        for b in range(blocks):
            later = scores(b + 1) if b + 1 < blocks else None
            absorb(b, *now)
            now = later
            if ch == CHUNKS - 1:
                finish(b)

    half = CHIPS // 2

    def got_copy(k):
        return pltpu.make_async_remote_copy(
            src_ref=got.at[core, k], dst_ref=got.at[core, k], send_sem=sib_ss.at[k], recv_sem=sib_rs.at[k],
            device_id=sibling, device_id_type=MESH,
        )

    def disp_arrive(k, carry):
        disp_copy(k, to_chip(k)).wait_recv()
        got_copy(k).start()
        return carry

    def got_wait(k, carry):
        got_copy(k).wait_recv()
        return carry

    def sum_copy(n, step):
        there = lax.rem(mp + step, 4)
        return pltpu.make_async_remote_copy(
            src_ref=part.at[n, pl.ds(pl.multiple_of(there * 32, 32), 32)], dst_ref=rsb.at[n, mp],
            send_sem=x_ss.at[n, step - 1], recv_sem=x_rs.at[n, step - 1], device_id=x_peer(step), device_id_type=MESH,
        )

    mine32 = pl.ds(pl.multiple_of(mp * 32, 32), 32)

    def hid_copy(n, step):
        return pltpu.make_async_remote_copy(
            src_ref=hid.at[n, mine32], dst_ref=hid.at[n, mine32],
            send_sem=x_ss.at[n, step + 2], recv_sem=x_rs.at[n, step + 2], device_id=x_peer(step), device_id_type=MESH,
        )

    def part_copy(n):
        return pltpu.make_async_remote_copy(
            src_ref=pxs.at[n], dst_ref=pxr.at[n], send_sem=sib_ss.at[CHIPS + n], recv_sem=sib_rs.at[CHIPS + n],
            device_id=sibling, device_id_type=MESH,
        )

    def ret_copy(k):
        return pltpu.make_async_remote_copy(
            src_ref=ret_s.at[k], dst_ref=ret_r.at[chip], send_sem=ret_ss.at[k], recv_sem=ret_rs.at[k],
            device_id=(from_chip(k) * 2 + core, mp), device_id_type=MESH,
        )

    def expert_up(n):
        if n == 0:
            got_copy(0).start()
        lax.fori_loop(max(1, n * half), n * half + half, disp_arrive, 0)
        if n == 0:
            load_gu.wait()
        lax.fori_loop(n * half, n * half + half, got_wait, 0)
        rows = jnp.concatenate([got[0, n * half : n * half + half], got[1, n * half : n * half + half]], axis=0)
        rows = rows.astype(F32).reshape(256, HALF).astype(BF)
        pr = iota((128, 256), 0)
        pc = iota((128, 256), 1)
        same = (pr // 4 == pc // 8) & (lax.rem(pr, 4) == lax.rem(pc, 4))
        left = dot(jnp.where(same & (lax.rem(pc // 4, 2) == 0), 1.0, 0.0).astype(BF), rows).astype(BF)
        right = dot(jnp.where(same & (lax.rem(pc // 4, 2) == 1), 1.0, 0.0).astype(BF), rows).astype(BF)
        part[n] = (dot(left, wgu[0:HALF, :]) + dot(right, wgu[HALF : 2 * HALF, :])).astype(BF)
        for step in (2, 1, 3):
            sum_copy(n, step).start()
        rsb[n, mp] = part[n, mine32, :]

    def expert_act(n):
        for step in (1, 2, 3):
            sum_copy(n, step).wait_recv()
        pre = rsb[n, 0].astype(F32) + rsb[n, 1].astype(F32) + rsb[n, 2].astype(F32) + rsb[n, 3].astype(F32)
        gate = pre[:, 0:512]
        hid[n, mine32, :] = (gate / (1.0 + jnp.exp(-gate)) * pre[:, 512:1024]).astype(BF)
        for step in (2, 1, 3):
            hid_copy(n, step).start()

    def expert_down(n):
        if n == 0:
            load_dn.wait()
        for step in (1, 2, 3):
            hid_copy(n, step).wait_recv()
        dr = iota((256, 128), 0)
        dc = iota((256, 128), 1)
        twice = jnp.where((dr // 8 == dc // 4) & (lax.rem(dr, 4) == lax.rem(dc, 4)), 1.0, 0.0).astype(BF)
        doubled = dot(twice, hid[n]).astype(BF)
        is_left = lax.rem(iota((256, HALF), 0) // 4, 2) == 0
        both = jnp.where(is_left, dot(doubled, wdn[:, 0:HALF]), dot(doubled, wdn[:, HALF : 2 * HALF]))
        pf[n] = both.reshape(2, 128, HALF)
        pxs[n] = pf[n, other].astype(BF)
        part_copy(n).start()

    def ret_start(k, carry):
        ret_copy(k).start()
        return carry

    def expert_back(n):
        part_copy(n).wait_recv()
        rows = slice(n * half, n * half + half)
        ret_s[rows] = (pf[n, core] + pxr[n].astype(F32)).reshape(half, 8, HALF).astype(BF)
        lax.fori_loop(max(1, n * half), n * half + half, ret_start, 0)
        if n == 0:
            ret_r[chip] = ret_s[0]

    def expert_mix():
        def ret_wait(k, carry):
            ret_copy(k).wait_recv()
            return carry

        lax.fori_loop(1, CHIPS, ret_wait, 0)
        rows256 = ret_r[...].astype(F32).reshape(256, HALF).astype(BF)
        weights = mixw[...]
        high = weights.astype(BF)
        low = (weights - high.astype(F32)).astype(BF)
        dims = (((0,), (0,)), ((), ()))
        mixed = lax.dot_general(high, rows256, dims, preferred_element_type=F32) + lax.dot_general(
            low, rows256, dims, preferred_element_type=F32
        )
        moe_v[:, 0:HALF] = mixed[0:64].astype(BF)
        moe_v[:, HALF : 2 * HALF] = mixed[64:128].astype(BF)


    order_copy.wait()
    expert_up(0)
    expert_up(1)
    expert_act(0)
    expert_act(1)
    arrivals(0)
    gather_chunk(0)
    arrivals(1)
    gather_chunk(1)
    arrivals(2)
    gather_chunk(2)
    expert_down(0)
    relay_chunk(0)
    expert_down(1)
    arrivals(3)
    gather_chunk(3)
    relay_chunk(1)
    arrivals(4)
    gather_chunk(4)
    expert_back(0)
    expert_back(1)
    relay_chunk(2)
    attend_chunk(0)
    relay_chunk(3)
    attend_chunk(1)
    relay_chunk(4)
    attend_chunk(2)
    attend_chunk(3)
    attend_chunk(4)
    expert_mix()

    def sent(k, carry):
        disp_copy(k, to_chip(k)).wait_send()
        page_copy(k, to_chip(k)).wait_send()
        forward_copy(k, from_chip(k)).wait_send()
        ret_copy(k).wait_send()
        got_copy(k).wait_send()
        return carry

    lax.fori_loop(1, CHIPS, sent, 0)
    forward_copy(0, chip).wait_send()
    got_copy(0).wait_send()
    for n in range(2):
        part_copy(n).wait_send()
        for step in (1, 2, 3):
            sum_copy(n, step).wait_send()
            hid_copy(n, step).wait_send()
    for ch in range(CHUNKS):
        for step in (1, 3):
            near_copy(ch, step).wait_send()
            far_copy(ch, step).wait_send()
    for b in range(ROWS // BLK):
        store_copy(b).wait()


def body(
    pool, send_slots, page_source, prefix_pages, queries, suffix_kv, hidden_in,
    expert_ids, expert_slots, gate_weights, w_gate_up, w_down,
):
    any_spec = pl.BlockSpec(memory_space=pl.ANY)
    vmem = pl.BlockSpec(memory_space=pltpu.VMEM)
    smem = pl.BlockSpec(memory_space=pltpu.SMEM)
    dma = pltpu.SemaphoreType.DMA
    scratch = [
        pltpu.VMEM((64, 9216), BF),
        pltpu.VMEM((64, 64, 128), BF),
        pltpu.VMEM((64, 16, 128), BF),
        pltpu.VMEM((CHIPS, 144, 128), BF),
        pltpu.VMEM((CHIPS, 144, 128), BF),
        pltpu.VMEM((CHIPS, 80, 128), BF),
        pltpu.VMEM((2, CHIPS, 80, 128), BF),
        pltpu.VMEM((CHUNKS, KEYS, WIDE), BF),
        pltpu.VMEM((ROWS, 640), BF),
        pltpu.VMEM((ROWS, 640), BF),
        pltpu.VMEM((64, 640), BF),
        pltpu.VMEM((ROWS, KVL), F32),
        pltpu.VMEM((ROWS, 128), F32),
        pltpu.VMEM((ROWS, 128), F32),
        pltpu.VMEM((64, HEADS * KVL), BF),
        pltpu.VMEM((64, HEADS * ENT), BF),
        pltpu.VMEM((2 * HALF, 1024), BF),
        pltpu.VMEM((512, 2 * HALF), BF),
        pltpu.VMEM((CHIPS, 8, HALF), BF),
        pltpu.VMEM((2, CHIPS, 8, HALF), BF),
        pltpu.VMEM((2, 128, 1024), BF),
        pltpu.VMEM((2, 4, 32, 1024), BF),
        pltpu.VMEM((2, 128, 512), BF),
        pltpu.VMEM((2, 2, 128, HALF), F32),
        pltpu.VMEM((2, 128, HALF), BF),
        pltpu.VMEM((2, 128, HALF), BF),
        pltpu.VMEM((CHIPS, 8, HALF), BF),
        pltpu.VMEM((CHIPS, 8, HALF), BF),
        pltpu.VMEM((256, 128), F32),
        pltpu.VMEM((8, 128), I32),
        pltpu.SMEM((8, 128), I32),
        dma((9,)),
        dma((CHIPS,)), dma((CHIPS,)),
        dma((CHIPS,)), dma((CHIPS,)),
        dma((CHIPS,)), dma((CHIPS,)),
        dma((CHIPS + 2,)), dma((CHIPS + 2,)),
        dma((2, 6)), dma((2, 6)),
        dma((CHIPS,)), dma((CHIPS,)),
        dma((CHUNKS, 4)), dma((CHUNKS, 4)),
    ]
    context, moe_out = pl.pallas_call(
        kernel,
        out_shape=(
            jax.ShapeDtypeStruct((64, HEADS * KVL), BF),
            jax.ShapeDtypeStruct((64, 2 * HALF), BF),
        ),
        in_specs=[any_spec, smem, vmem, smem, any_spec, vmem, vmem, vmem, vmem, vmem, any_spec, any_spec],
        out_specs=(any_spec, vmem),
        scratch_shapes=scratch,
        compiler_params=pltpu.CompilerParams(
            collective_id=0, has_side_effects=True, vmem_limit_bytes=56 * 2**20
        ),
        name="prefill",
    )(
        pool, send_slots, page_source, prefix_pages, queries, suffix_kv, hidden_in,
        expert_ids.T, expert_slots.T, gate_weights.T, w_gate_up, w_down,
    )
    return context, moe_out


def solution(mesh):
    return jax.shard_map(
        body,
        mesh=mesh,
        in_specs=(
            P("dp", "mp"),
            P("dp", None),
            P("dp", None),
            P("dp"),
            P("dp", "mp"),
            P("dp", None),
            P("dp", "mp"),
            P("dp", None),
            P("dp", None),
            P("dp", None),
            P("dp", "mp", None),
            P("dp", None, "mp"),
        ),
        out_specs=(P("dp", "mp"), P("dp", "mp")),
        check_vma=False,
    )
```
